32 devices in a mesh: groups: 2 (over y), pool: 8 (over z, x), tp: 2 (over core).
Axes of the slice: x: 2, y: 2, z: 4, core: 2. Of those that a mesh axis runs over, the one named last changes fastest.
Arguments:
- queries: bfloat16 [4096, 8192], P(('groups', 'pool'), 'tp'), parts along dimension 0, may hold values from -10 to 10
- new_keys: bfloat16 [4096, 1024], P(('groups', 'pool'), 'tp'), parts along dimension 0, may hold values from -5 to 5
- new_values: bfloat16 [4096, 1024], P(('groups', 'pool'), 'tp'), parts along dimension 0, may hold values from -6 to 6
- key_pool: bfloat16 [2048, 16, 1024], P(('groups', 'pool'), None, 'tp'), parts along dimension 0, may hold values from -4 to 4
- value_pool: bfloat16 [2048, 16, 1024], P(('groups', 'pool'), None, 'tp'), parts along dimension 0, may hold values from -4 to 4
- page_key_scale: bfloat16 [2048, 8], P(('groups', 'pool'), 'tp'), parts along dimension 0, may hold values from 0.5 to 2
- value_scale: bfloat16 [2048, 8], P(('groups', 'pool'), 'tp'), parts along dimension 0, may hold values from 0.5 to 2
- page_owner: int32 [16, 128], P(('groups', 'pool')), parts along dimension 0, may hold values from 0 to 7, as said below
- page_slot: int32 [16, 128], P(('groups', 'pool')), parts along dimension 0, may hold values from 0 to 127, as said below
- prefix_len: int32 [16], P(('groups', 'pool')), parts along dimension 0, may hold values from 1 to 2048, 8192 in all
- dec_owner: int32 [16, 256], P(('groups', 'pool')), parts along dimension 0, may hold values from 0 to 7, as said below
- dec_slot: int32 [16, 256], P(('groups', 'pool')), parts along dimension 0, may hold values from 0 to 511, as said below
- decode_keys: bfloat16 [8192, 1024], P(('groups', 'pool'), 'tp'), parts along dimension 0, may hold values from -6 to 6
- decode_values: bfloat16 [8192, 1024], P(('groups', 'pool'), 'tp'), parts along dimension 0, may hold values from -6 to 6
Outputs:
- attended: bfloat16 [4096, 8192], P(('groups', 'pool'), 'tp'), parts along dimension 0
- decode_keys_out: bfloat16 [8192, 1024], P(('groups', 'pool'), 'tp'), parts along dimension 0
- decode_values_out: bfloat16 [8192, 1024], P(('groups', 'pool'), 'tp'), parts along dimension 0
The draws below stay inside these ranges and needn't reach their ends.
There are 2 independent parts, one for each index of `groups`. The reference program is written for one: setup_inputs(seed, part) draws one part's arguments, and reference() takes and returns one part's arrays. A program takes and returns all parts, laid end to end along the dimension named above; each array names one. Nothing has to cross between parts.
Inputs may be any that keep to these rules, and one draw needn't show every extreme that they name: `page_owner`: each request has exactly 16 of its pages on every owner. `page_slot`: pages that share an owner have different slots. `dec_owner`: each request sends exactly 32 of its new rows to every decode owner. `dec_slot`: new rows that share a decode owner have different slots, and each owner's slot 511 receives a row.
All inputs are finite; a program needn't handle non-finite values. No bound on the sum of `prefix_len` on one device may be relied on, other than what follows from the above.
Results may differ from the reference program's by a relative error of at most 0.0089.
Values may be sent and summed in bfloat16 or wider, within the bound.
A program may use at most 64 MiB of HBM per device.

```python
import math
import jax
import jax.numpy as jnp
import numpy as np
from jax import lax

QH = 64
KVH = 8
HD = 128
SPAN = 256
PAGE_TOK = 16
PAGES_REQ = 128
REQS = 8
PREFIX = 2048
CAP = 16
CAP_ROWS = 32
DEC_ROWS = 512
TOKENS = 2048


def permute_rows(key, count, length):

    def single(one_key):
        return jax.random.permutation(one_key, length)
    return jax.vmap(single)(jax.random.split(key, count)).astype(jnp.int32)


def page_tables(key):
    order_key, slot_key = jax.random.split(key)
    order = permute_rows(order_key, REQS, PAGES_REQ)
    owner = order // CAP
    within = order % CAP
    owner_slots = permute_rows(slot_key, REQS, PAGES_REQ)
    requests = jnp.arange(REQS, dtype=jnp.int32)[:, None]
    slot = owner_slots[owner, requests * CAP + within]
    return (owner.astype(jnp.int32), slot.astype(jnp.int32))


def row_tables(key):
    order_key, slot_key = jax.random.split(key)
    order = permute_rows(order_key, REQS, SPAN)
    owner = order // CAP_ROWS
    within = order % CAP_ROWS
    chosen = permute_rows(slot_key, REQS, DEC_ROWS)[:, :SPAN]
    has_last = jnp.any(chosen == DEC_ROWS - 1, axis=1)
    chosen = chosen.at[:, 0].set(jnp.where(has_last, chosen[:, 0], DEC_ROWS - 1))
    requests = jnp.arange(REQS, dtype=jnp.int32)[:, None]
    slot = chosen[owner, requests * CAP_ROWS + within]
    return (owner.astype(jnp.int32), slot.astype(jnp.int32))


def draw_queries(key, part):
    key = jax.random.fold_in(key, 3)
    values = jnp.clip(2.5 * jax.random.normal(key, (REQS * SPAN, QH * HD)), -10.0, 10.0)
    return values.astype(jnp.bfloat16)


def draw_new_keys(key, part):
    key = jax.random.fold_in(key, 5)
    values = jnp.clip(jax.random.normal(key, (REQS * SPAN, KVH * HD)), -4.5, 4.5)
    return values.astype(jnp.bfloat16)


def draw_page_owner(key, part):
    owner, slot = page_tables(key)
    return owner


def draw_page_slot(key, part):
    owner, slot = page_tables(key)
    return slot


def draw_dec_owner(key, part):
    owner, slot = row_tables(jax.random.fold_in(key, 21))
    return owner


def draw_dec_slot(key, part):
    owner, slot = row_tables(jax.random.fold_in(key, 21))
    return slot


def shard_levels(own_key, extent, shards, least, top_value):
    factor_of, own = 1.0, jax.random.fold_in(own_key, 6)
    for axis_at, shards_of in shards:
        draws = jnp.exp(jax.random.uniform(jax.random.fold_in(own, axis_at), (shards_of,), jnp.float32, least / len(shards), top_value / len(shards)))
        factor_of = factor_of * jnp.repeat(draws, extent[axis_at] // shards_of).reshape([-1 if axis == axis_at else 1 for axis in range(len(extent))])
    return factor_of


def split_up(amount, total, limit, lean):
    portions = [(1 << 20) // math.isqrt(rank ** lean) + 1 for rank in range(2, amount + 1)]
    surplus, counts = total - limit - (amount - 1), [1] * (amount - 1)
    while surplus > 0:
        candidates = [i for i in range(amount - 1) if counts[i] < limit]
        mass, budget = sum([portions[i] for i in candidates]), surplus
        for i in candidates:
            more = min(limit - counts[i], max(1, budget * portions[i] // mass), surplus)
            counts[i] = counts[i] + more
            surplus = surplus - more
    return np.array([limit] + counts)


def ragged_sizes(stream_key, count, total, most, slope):
    if count == 2:
        one = jax.random.randint(stream_key, (), max(1, total - most), min(most, total - 1) + 1)
        return jnp.stack([one, total - one])
    tallies = jnp.asarray(split_up(count, total, most, slope), jnp.int32)
    couples = (count - 1) // 2
    donor, taker = tallies[1:1 + 2 * couples:2], tallies[2:2 + 2 * couples:2]
    margin = jnp.minimum(donor - 1, most - taker)
    passed = jax.random.randint(jax.random.fold_in(stream_key, 1), (couples,), 0, 1 << 20) % (margin + 1)
    tallies = tallies.at[1:1 + 2 * couples:2].set(donor - passed).at[2:2 + 2 * couples:2].set(taker + passed)
    return tallies[jax.random.permutation(jax.random.fold_in(stream_key, 2), count)]


def gaussian(stream_key, dims, scale, reach, cuts=(), kind=jnp.bfloat16):
    array = scale * jax.random.normal(stream_key, dims, jnp.float32)
    if cuts:
        array = array * shard_levels(stream_key, dims, cuts, -0.22, 0.18)
    return jnp.clip(array, -reach, reach).astype(kind)


def setup_inputs(seed: int = 0, part: int = 0) -> dict:
    seeds = jax.random.split(jax.random.key(seed), 15)
    own_keys = jax.random.split(jax.random.fold_in(seeds[14], part), 15)
    queries = draw_queries(jax.random.fold_in(jax.random.fold_in(seeds[14], part), 71), part)
    new_keys = draw_new_keys(jax.random.fold_in(jax.random.fold_in(seeds[14], part), 71), part)
    new_values = gaussian(own_keys[2], (TOKENS, KVH * HD), 1.0, 6.0, ((0, 8), (1, 2)))
    key_pool = gaussian(own_keys[3], (REQS * PAGES_REQ, PAGE_TOK, KVH * HD), 1.0, 4.0, ((0, 8), (2, 2)))
    value_pool = gaussian(own_keys[4], (REQS * PAGES_REQ, PAGE_TOK, KVH * HD), 1.0, 4.0, ((0, 8), (2, 2)))
    page_key_scale = jnp.clip(jnp.exp(math.log(2.0) - 1.3862944 * jax.random.uniform(own_keys[5], (REQS * PAGES_REQ, KVH), jnp.float32) ** shard_levels(own_keys[5], (REQS * PAGES_REQ, KVH), ((0, 8), (1, 2)), -0.2, 0.2)), 0.5, 2.0).astype(jnp.bfloat16)
    value_scale = jnp.clip(jnp.exp(math.log(2.0) - 1.3862944 * jax.random.uniform(own_keys[6], (REQS * PAGES_REQ, KVH), jnp.float32) ** shard_levels(own_keys[6], (REQS * PAGES_REQ, KVH), ((0, 8), (1, 2)), -0.2, 0.2)), 0.5, 2.0).astype(jnp.bfloat16)
    page_owner = draw_page_owner(jax.random.fold_in(jax.random.fold_in(seeds[14], part), 71), part)
    page_slot = draw_page_slot(jax.random.fold_in(jax.random.fold_in(seeds[14], part), 71), part)
    prefix_len = ragged_sizes(own_keys[9], REQS, REQS * PREFIX // 2, PREFIX, 2).astype(jnp.int32)
    dec_owner = draw_dec_owner(jax.random.fold_in(jax.random.fold_in(seeds[14], part), 71), part)
    dec_slot = draw_dec_slot(jax.random.fold_in(jax.random.fold_in(seeds[14], part), 71), part)
    decode_keys = gaussian(own_keys[12], (REQS * DEC_ROWS, KVH * HD), 1.0, 6.0, ((0, 8), (1, 2)))
    decode_values = gaussian(own_keys[13], (REQS * DEC_ROWS, KVH * HD), 1.0, 6.0, ((0, 8), (1, 2)))
    return {"queries": queries, "new_keys": new_keys, "new_values": new_values, "key_pool": key_pool, "value_pool": value_pool, "page_key_scale": page_key_scale, "value_scale": value_scale, "page_owner": page_owner, "page_slot": page_slot, "prefix_len": prefix_len, "dec_owner": dec_owner, "dec_slot": dec_slot, "decode_keys": decode_keys, "decode_values": decode_values}


def dequantize(codes, scales, count_of_heads):
    count, page_tok, columns = codes.shape
    spread = codes.astype(jnp.float32).reshape(count, page_tok, count_of_heads, columns // count_of_heads)
    scaled = spread * scales.astype(jnp.float32)[:, None, :, None]
    return scaled.astype(jnp.bfloat16).reshape(count * page_tok, columns)

def head_attend(query_block, pre_keys, pre_values, fresh_keys, fresh_values, length):
    factor = 1.0 / math.sqrt(query_block.shape[2])
    query_wide = query_block.astype(jnp.float32)
    pre_scores = jnp.einsum('tgd,kd->gtk', query_wide, pre_keys.astype(jnp.float32)) * factor
    new_scores = jnp.einsum('tgd,kd->gtk', query_wide, fresh_keys.astype(jnp.float32)) * factor
    pre_seen = (jnp.arange(pre_keys.shape[0], dtype=jnp.int32) < length)[None, None, :]
    positions = jnp.arange(query_block.shape[0], dtype=jnp.int32)
    causal = (positions[:, None] >= positions[None, :])[None]
    pre_scores = jnp.where(pre_seen, pre_scores, -jnp.inf)
    new_scores = jnp.where(causal, new_scores, -jnp.inf)
    row_max = jnp.maximum(lax.optimization_barrier(jnp.max(pre_scores, axis=2)), lax.optimization_barrier(jnp.max(new_scores, axis=2)))[:, :, None]
    pre_weights = jnp.exp(pre_scores - row_max)
    new_weights = jnp.exp(new_scores - row_max)
    row_total = lax.optimization_barrier(jnp.sum(pre_weights, axis=2)) + lax.optimization_barrier(jnp.sum(new_weights, axis=2))
    pre_rounded = lax.optimization_barrier(pre_weights.astype(jnp.bfloat16)).astype(jnp.float32)
    new_rounded = lax.optimization_barrier(new_weights.astype(jnp.bfloat16)).astype(jnp.float32)
    summed = jnp.einsum('gtk,kd->tgd', pre_rounded, pre_values.astype(jnp.float32))
    summed = summed + jnp.einsum('gtk,kd->tgd', new_rounded, fresh_values.astype(jnp.float32))
    return (summed / jnp.transpose(row_total)[:, :, None]).astype(jnp.bfloat16)

def reference(queries, new_keys, new_values, key_pool, value_pool, page_key_scale, value_scale, page_owner, page_slot, prefix_len, dec_owner, dec_slot, decode_keys, decode_values):
    page_index = (page_owner * PAGES_REQ + page_slot).astype(jnp.int32)
    group_size = QH // KVH

    def one_request(request):
        rows = page_index[request]
        pre_keys = dequantize(key_pool[rows], page_key_scale[rows], KVH)
        pre_values = dequantize(value_pool[rows], value_scale[rows], KVH)
        start = (request * SPAN).astype(jnp.int32)
        query_rows = lax.dynamic_slice_in_dim(queries, start, SPAN, 0)
        fresh_keys = lax.dynamic_slice_in_dim(new_keys, start, SPAN, 0)
        fresh_values = lax.dynamic_slice_in_dim(new_values, start, SPAN, 0)
        length = prefix_len[request]

        def one_head(head):
            offset = (head * HD).astype(jnp.int32)
            query_cols = lax.dynamic_slice_in_dim(query_rows, (head * group_size * HD).astype(jnp.int32), group_size * HD, 1)
            query_block = query_cols.reshape(SPAN, group_size, HD)
            result = head_attend(query_block, lax.dynamic_slice_in_dim(pre_keys, offset, HD, 1), lax.dynamic_slice_in_dim(pre_values, offset, HD, 1), lax.dynamic_slice_in_dim(fresh_keys, offset, HD, 1), lax.dynamic_slice_in_dim(fresh_values, offset, HD, 1), length)
            return result.reshape(SPAN, group_size * HD)
        per_head = lax.map(one_head, jnp.arange(KVH, dtype=jnp.int32))
        return jnp.transpose(per_head, (1, 0, 2)).reshape(SPAN, QH * HD)
    attended = lax.map(one_request, jnp.arange(REQS, dtype=jnp.int32)).reshape(REQS * SPAN, QH * HD)
    target = (dec_owner * DEC_ROWS + dec_slot).astype(jnp.int32).reshape(REQS * SPAN)
    decode_keys_out = decode_keys.at[target].set(new_keys)
    decode_values_out = decode_values.at[target].set(new_values)
    return (attended, decode_keys_out, decode_values_out)
```

```python
import functools
import math

import jax
import jax.numpy as jnp
from jax import lax
from jax.experimental import pallas as pl
from jax.experimental.pallas import tpu as pltpu
from jax.sharding import PartitionSpec as P

MESH = pl.DeviceIdType.MESH
LOW = -1e30
TABLE_ROWS_AT = 64
UNROLL = 4


def flipped(me, d):
    out = me
    bit = 1
    while bit <= d:
        if d & bit:
            out = out + bit - 2 * bit * lax.rem(lax.div(me, bit), 2)
        bit *= 2
    return out


def send_order(n):
    top = n // 2
    order = []
    while top >= 1:
        order += list(range(top, 2 * top))
        top //= 2
    return order


def kernel(
    n,
    rows,
    page_tok,
    dec_rows,
    dec_pad,
    kv_heads,
    group,
    tab_ref,
    placed_ref,
    q_ref,
    nk_ref,
    nv_ref,
    kp_ref,
    vp_ref,
    ks_ref,
    vs_ref,
    bias_ref,
    out_ref,
    come_ref,
    tabin_ref,
    tab_smem,
    stage,
    recv,
    push,
    acc,
    m_ref,
    l_ref,
    tsend,
    trecv,
    psend,
    precv,
    dsend,
    drecv,
    lsem,
):
    me = lax.axis_index("pool")
    keys = rows * page_tok
    span = q_ref.shape[0]
    heads = kv_heads * group
    hd = q_ref.shape[1] // heads
    order = send_order(n)

    barrier = pltpu.get_barrier_semaphore()
    for d in range(1, n):
        pl.semaphore_signal(barrier, inc=1, device_id={"pool": flipped(me, d)}, device_id_type=MESH)
    pl.semaphore_wait(barrier, n - 1)

    def table_copy(d):
        p = flipped(me, d)
        return pltpu.make_async_remote_copy(
            src_ref=tab_ref.at[p],
            dst_ref=tabin_ref.at[me],
            send_sem=tsend.at[d],
            recv_sem=trecv.at[d],
            device_id={"pool": p},
            device_id_type=MESH,
        )

    def page_copy(d):
        return pltpu.make_async_remote_copy(
            src_ref=stage.at[d],
            dst_ref=recv.at[:, pl.ds(pl.multiple_of(me * keys, keys), keys)],
            send_sem=psend.at[d],
            recv_sem=precv.at[d],
            device_id={"pool": flipped(me, d)},
            device_id_type=MESH,
        )

    def row_copy(d):
        p = flipped(me, d)
        return pltpu.make_async_remote_copy(
            src_ref=push.at[p],
            dst_ref=come_ref.at[me],
            send_sem=dsend.at[d],
            recv_sem=drecv.at[d],
            device_id={"pool": p},
            device_id_type=MESH,
        )

    for d in order:
        table_copy(d).start()
    tabin_ref[me] = tab_ref[me]
    for d in order:
        table_copy(d).wait_recv()
    to_smem = pltpu.make_async_copy(tabin_ref, tab_smem, lsem)
    to_smem.start()
    to_smem.wait()

    def gather(p, write):
        def one(k, carry):
            slot = tab_smem[p, 0, k]
            at = pl.multiple_of(k * page_tok, page_tok)
            key_page = kp_ref[slot].astype(jnp.float32) * ks_ref[slot]
            value_page = vp_ref[slot].astype(jnp.float32) * vs_ref[slot]
            write(at, key_page.astype(jnp.bfloat16), value_page.astype(jnp.bfloat16))
            return carry

        lax.fori_loop(0, rows, one, 0, unroll=True)

    for d in order:

        def to_stage(at, key_page, value_page):
            stage[d, 0, pl.ds(at, page_tok)] = key_page
            stage[d, 1, pl.ds(at, page_tok)] = value_page

        gather(flipped(me, d), to_stage)
        page_copy(d).start()

    def to_own(at, key_page, value_page):
        base = pl.multiple_of(me * keys, keys)
        recv[0, pl.ds(base + at, page_tok)] = key_page
        recv[1, pl.ds(base + at, page_tok)] = value_page

    gather(me, to_own)

    for o in range(n):
        spot = lax.broadcasted_iota(jnp.int32, (dec_pad, span), 0) + o * dec_pad
        placed = placed_ref[...]
        pick_k = jnp.where(spot == placed, 1.0, 0.0).astype(jnp.bfloat16)
        pick_v = jnp.where(spot == placed + dec_rows, 1.0, 0.0).astype(jnp.bfloat16)
        push[o] = (
            jnp.dot(pick_k, nk_ref[...], preferred_element_type=jnp.float32)
            + jnp.dot(pick_v, nv_ref[...], preferred_element_type=jnp.float32)
        ).astype(jnp.bfloat16)
    come_ref[me] = push[me]
    for d in order:
        row_copy(d).start()

    scale = math.log2(math.e) / math.sqrt(hd)

    def attend(load_k, load_v, load_bias, first):
        def some_heads(i, carry):
            for u in range(UNROLL):
                c = i * UNROLL + u
                h = lax.div(i * UNROLL, group)
                col = pl.multiple_of(h * hd, hd)
                q = q_ref[:, pl.ds(pl.multiple_of(c * hd, hd), hd)]
                s = lax.dot_general(
                    load_k(col), q, (((1,), (1,)), ((), ())), preferred_element_type=jnp.float32
                )
                s = s + load_bias()
                top = jnp.max(s, axis=0, keepdims=True)
                if not first:
                    old = m_ref[c]
                    top = jnp.maximum(old, top)
                w = jnp.exp2((s - top) * scale)
                part = jnp.sum(w.reshape(w.shape[0] // 8, 8, span), axis=0)
                summed = lax.dot_general(
                    load_v(col),
                    w.astype(jnp.bfloat16),
                    (((0,), (0,)), ((), ())),
                    preferred_element_type=jnp.float32,
                )
                if first:
                    l_ref[c] = part
                    acc[c] = summed
                else:
                    fade = jnp.exp2((old - top) * scale)
                    l_ref[c] = l_ref[c] * fade + part
                    acc[c] = acc[c] * fade + summed
                m_ref[c] = top
            return carry

        lax.fori_loop(0, heads // UNROLL, some_heads, 0)

    def causal():
        s_at = lax.broadcasted_iota(jnp.int32, (span, span), 0)
        t_at = lax.broadcasted_iota(jnp.int32, (span, span), 1)
        return jnp.where(s_at <= t_at, 0.0, LOW)

    attend(lambda col: nk_ref[:, pl.ds(col, hd)], lambda col: nv_ref[:, pl.ds(col, hd)], causal, True)

    per_block = max(1, 256 // keys)
    block = per_block * keys
    own_block = lax.div(me, per_block)
    done = {0}
    for i in [0] + send_order(n // per_block):
        for d in range(i * per_block, (i + 1) * per_block):
            if d:
                page_copy(d).wait_recv()
        base = pl.multiple_of(flipped(own_block, i) * block, block)

        def bias_block():
            b = bias_ref[pl.ds(base, block), :]
            return jnp.concatenate([b] * (span // b.shape[1]), axis=1)

        attend(
            lambda col: recv[0, pl.ds(base, block), pl.ds(col, hd)],
            lambda col: recv[1, pl.ds(base, block), pl.ds(col, hd)],
            bias_block,
            False,
        )

    def finish(c, carry):
        total = jnp.sum(l_ref[c], axis=0, keepdims=True)
        value = acc[c] / total
        out_ref[:, pl.ds(pl.multiple_of(c * hd, hd), hd)] = value.T.astype(jnp.bfloat16)
        return carry

    lax.fori_loop(0, heads, finish, 0)

    for d in order:
        table_copy(d).wait_send()
        page_copy(d).wait_send()
        row_copy(d).wait()


def ranks(owner):
    at = jnp.arange(owner.shape[0], dtype=jnp.int32)
    same = owner[:, None] == owner[None, :]
    return jnp.sum(same & (at[None, :] < at[:, None]), axis=1, dtype=jnp.int32)


def shards(
    queries,
    new_keys,
    new_values,
    key_pool,
    value_pool,
    page_key_scale,
    value_scale,
    page_owner,
    page_slot,
    prefix_len,
    dec_owner,
    dec_slot,
    decode_keys,
    decode_values,
):
    n = lax.axis_size("pool")
    page_count = page_owner.shape[1]
    rows = page_count // n
    span = queries.shape[0]
    dec_rows = span // n
    dec_pad = -(-2 * dec_rows // 16) * 16
    columns = new_keys.shape[1]
    kv_heads = page_key_scale.shape[1]
    hd = columns // kv_heads
    group = queries.shape[1] // columns
    pool_pages, page_tok, _ = key_pool.shape
    keys = rows * page_tok

    owner, slot = page_owner[0], page_slot[0]
    place = owner * rows + ranks(owner)
    hit = place[None, :] == jnp.arange(page_count, dtype=jnp.int32)[:, None]
    slots = jnp.sum(jnp.where(hit, slot[None, :], 0), axis=1).reshape(n, rows)
    pages = jnp.sum(
        jnp.where(hit, jnp.arange(page_count, dtype=jnp.int32)[None, :], 0), axis=1
    )
    position = pages[:, None] * page_tok + jnp.arange(page_tok, dtype=jnp.int32)[None, :]
    bias = jnp.where(position.reshape(page_count * page_tok) < prefix_len[0], 0.0, LOW)
    bias = jnp.broadcast_to(bias.astype(jnp.float32)[:, None], (page_count * page_tok, 128))

    d_owner, d_slot = dec_owner[0], dec_slot[0]
    d_rank = ranks(d_owner)
    d_hit = (d_owner * dec_rows + d_rank)[None, :] == jnp.arange(span, dtype=jnp.int32)[:, None]
    d_slots = jnp.sum(jnp.where(d_hit, d_slot[None, :], 0), axis=1).reshape(n, dec_rows)
    placed = (d_owner * dec_pad + d_rank)[None, :]

    table = jnp.concatenate(
        [
            slots,
            jnp.zeros((n, TABLE_ROWS_AT - rows), jnp.int32),
            d_slots,
            jnp.zeros((n, 128 - TABLE_ROWS_AT - dec_rows), jnp.int32),
        ],
        axis=1,
    ).reshape(n, 1, 128)
    key_scale = jnp.repeat(page_key_scale.astype(jnp.float32), hd, axis=1)[:, None, :]
    val_scale = jnp.repeat(value_scale.astype(jnp.float32), hd, axis=1)[:, None, :]

    heads = kv_heads * group
    vmem = pl.BlockSpec(memory_space=pltpu.VMEM)
    attended, come, table_in = pl.pallas_call(
        functools.partial(
            kernel, n, rows, page_tok, dec_rows, dec_pad, kv_heads, group
        ),
        out_shape=(
            jax.ShapeDtypeStruct(queries.shape, jnp.bfloat16),
            jax.ShapeDtypeStruct((n, dec_pad, columns), jnp.bfloat16),
            jax.ShapeDtypeStruct((n, 1, 128), jnp.int32),
        ),
        in_specs=[vmem] * 10,
        out_specs=(vmem, vmem, vmem),
        scratch_shapes=[
            pltpu.SMEM((n, 1, 128), jnp.int32),
            pltpu.VMEM((n, 2, keys, columns), jnp.bfloat16),
            pltpu.VMEM((2, n * keys, columns), jnp.bfloat16),
            pltpu.VMEM((n, dec_pad, columns), jnp.bfloat16),
            pltpu.VMEM((heads, hd, span), jnp.float32),
            pltpu.VMEM((heads, 1, span), jnp.float32),
            pltpu.VMEM((heads, 8, span), jnp.float32),
            pltpu.SemaphoreType.DMA((n,)),
            pltpu.SemaphoreType.DMA((n,)),
            pltpu.SemaphoreType.DMA((n,)),
            pltpu.SemaphoreType.DMA((n,)),
            pltpu.SemaphoreType.DMA((n,)),
            pltpu.SemaphoreType.DMA((n,)),
            pltpu.SemaphoreType.DMA,
        ],
        compiler_params=pltpu.CompilerParams(
            collective_id=0, has_side_effects=True, vmem_limit_bytes=52 * 1024 * 1024
        ),
        cost_estimate=pl.CostEstimate(
            flops=4 * span * heads * hd * (n * keys + span),
            bytes_accessed=16 * 1024 * 1024,
            transcendentals=span * heads * (n * keys + span),
        ),
    )(
        table,
        placed,
        queries,
        new_keys,
        new_values,
        key_pool,
        value_pool,
        key_scale,
        val_scale,
        bias,
    )

    come_slot = table_in[:, 0, TABLE_ROWS_AT : TABLE_ROWS_AT + dec_rows].reshape(span)
    put = jnp.arange(decode_keys.shape[0], dtype=jnp.int32)[:, None] == come_slot[None, :]
    touched = jnp.any(put, axis=1)[:, None]
    put = put.astype(jnp.bfloat16)
    come_keys = come[:, :dec_rows].reshape(span, columns)
    come_values = come[:, dec_rows : 2 * dec_rows].reshape(span, columns)
    keys_out = jnp.where(
        touched,
        jnp.dot(put, come_keys, preferred_element_type=jnp.float32).astype(jnp.bfloat16),
        decode_keys,
    )
    values_out = jnp.where(
        touched,
        jnp.dot(put, come_values, preferred_element_type=jnp.float32).astype(jnp.bfloat16),
        decode_values,
    )
    return attended, keys_out, values_out


def solution(mesh):
    two = P(("groups", "pool"), "tp")
    three = P(("groups", "pool"), None, "tp")
    table = P(("groups", "pool"), None)
    in_specs = (two, two, two, three, three, two, two, table, table)
    in_specs += (P(("groups", "pool")), table, table, two, two)
    return jax.shard_map(
        shards, mesh=mesh, in_specs=in_specs, out_specs=(two, two, two), check_vma=False
    )
```

```python
import functools
import math

import jax
import jax.numpy as jnp
from jax import lax
from jax.experimental import pallas as pl
from jax.experimental.pallas import tpu as pltpu
from jax.sharding import PartitionSpec as P

MESH = pl.DeviceIdType.MESH
LOW = -1e30
TABLE_ROWS_AT = 64
UNROLL = 8


def flipped(me, d):
    out = me
    bit = 1
    while bit <= d:
        if d & bit:
            out = out + bit - 2 * bit * lax.rem(lax.div(me, bit), 2)
        bit *= 2
    return out


def send_order(n):
    top = n // 2
    order = []
    while top >= 1:
        order += list(range(top, 2 * top))
        top //= 2
    return order


def kernel(
    n,
    rows,
    page_tok,
    dec_rows,
    dec_pad,
    kv_heads,
    group,
    tab_ref,
    placed_ref,
    q_ref,
    nk_ref,
    nv_ref,
    kp_ref,
    vp_ref,
    ks_ref,
    vs_ref,
    bias_ref,
    out_ref,
    come_ref,
    tabin_ref,
    tab_smem,
    stage,
    recv,
    push,
    qs_ref,
    acc,
    m_ref,
    tsend,
    trecv,
    psend,
    precv,
    dsend,
    drecv,
    lsem,
):
    me = lax.axis_index("pool")
    keys = rows * page_tok
    span = q_ref.shape[0]
    heads = kv_heads * group
    hd = q_ref.shape[1] // heads
    order = send_order(n)

    barrier = pltpu.get_barrier_semaphore()
    for d in range(1, n):
        pl.semaphore_signal(barrier, inc=1, device_id={"pool": flipped(me, d)}, device_id_type=MESH)
    pl.semaphore_wait(barrier, n - 1)

    def table_copy(d):
        p = flipped(me, d)
        return pltpu.make_async_remote_copy(
            src_ref=tab_ref.at[p],
            dst_ref=tabin_ref.at[me],
            send_sem=tsend.at[d],
            recv_sem=trecv.at[d],
            device_id={"pool": p},
            device_id_type=MESH,
        )

    def page_copy(d, half):
        return pltpu.make_async_remote_copy(
            src_ref=stage.at[d, half],
            dst_ref=recv.at[half, pl.ds(pl.multiple_of(me * keys, keys), keys)],
            send_sem=psend.at[half, d],
            recv_sem=precv.at[half, d],
            device_id={"pool": flipped(me, d)},
            device_id_type=MESH,
        )

    def row_copy(d):
        p = flipped(me, d)
        return pltpu.make_async_remote_copy(
            src_ref=push.at[p],
            dst_ref=come_ref.at[me],
            send_sem=dsend.at[d],
            recv_sem=drecv.at[d],
            device_id={"pool": p},
            device_id_type=MESH,
        )

    for d in order:
        table_copy(d).start()
    tabin_ref[me] = tab_ref[me]
    for d in order:
        table_copy(d).wait_recv()
    to_smem = pltpu.make_async_copy(tabin_ref, tab_smem, lsem)
    to_smem.start()
    to_smem.wait()

    def gather(p, write):
        def one(k, carry):
            slot = tab_smem[p, 0, k]
            at = pl.multiple_of(k * page_tok, page_tok)
            key_page = kp_ref[slot].astype(jnp.float32) * ks_ref[slot]
            value_page = vp_ref[slot].astype(jnp.float32) * vs_ref[slot]
            write(at, key_page.astype(jnp.bfloat16), value_page.astype(jnp.bfloat16))
            return carry

        lax.fori_loop(0, rows, one, 0, unroll=True)

    per_block = max(1, 256 // keys)
    block = per_block * keys
    far = list(range(n // 2, n))
    near = list(range(1, n // 2))
    queue = [(d, half) for d in far for half in range(2)]
    window = min(len(queue), 3 * per_block)
    ahead = list(range(n // 2, n // 2 + -(-window // 2)))

    def gather_for(d):
        def to_stage(at, key_page, value_page):
            stage[d, 0, pl.ds(at, page_tok)] = key_page
            stage[d, 1, pl.ds(at, page_tok)] = value_page

        gather(flipped(me, d), to_stage)

    for d in ahead:
        gather_for(d)
        for half in range(2):
            if (d, half) in queue[:window]:
                page_copy(d, half).start()
    for d in near:
        gather_for(d)
        page_copy(d, 0).start()
        page_copy(d, 1).start()
    for d in far:
        if d not in ahead:
            gather_for(d)

    def to_own(at, key_page, value_page):
        base = pl.multiple_of(me * keys, keys)
        recv[0, pl.ds(base + at, page_tok)] = key_page
        recv[1, pl.ds(base + at, page_tok)] = value_page

    gather(me, to_own)

    for o in range(n):
        spot = lax.broadcasted_iota(jnp.int32, (dec_pad, span), 0) + o * dec_pad
        placed = placed_ref[...]
        pick_k = jnp.where(spot == placed, 1.0, 0.0).astype(jnp.bfloat16)
        pick_v = jnp.where(spot == placed + dec_rows, 1.0, 0.0).astype(jnp.bfloat16)
        push[o] = (
            jnp.dot(pick_k, nk_ref[...], preferred_element_type=jnp.float32)
            + jnp.dot(pick_v, nv_ref[...], preferred_element_type=jnp.float32)
        ).astype(jnp.bfloat16)
    come_ref[me] = push[me]
    for d in order:
        row_copy(d).start()

    scale = math.log2(math.e) / math.sqrt(hd)

    rows_q = UNROLL * span

    def turn(c, carry):
        qs_ref[pl.ds(pl.multiple_of(c * span, span), span)] = q_ref[
            :, pl.ds(pl.multiple_of(c * hd, hd), hd)
        ]
        return carry

    lax.fori_loop(0, heads, turn, 0)

    def attend(load_k, load_v, load_bias, first):
        def some_heads(i, carry):
            h = lax.div(i * UNROLL, group)
            col = pl.multiple_of(h * hd, hd)
            at = pl.ds(pl.multiple_of(i * rows_q, rows_q), rows_q)
            k_now, v_now = load_k(col), load_v(col)
            v_now = jnp.concatenate([v_now, jnp.ones_like(v_now)], axis=1)
            s = lax.dot_general(
                qs_ref[at], k_now, (((1,), (1,)), ((), ())), preferred_element_type=jnp.float32
            )
            s = s + load_bias()
            top = jnp.broadcast_to(jnp.max(s, axis=1, keepdims=True), (rows_q, hd))
            if not first:
                old = m_ref[at]
                top = jnp.maximum(old, top)
            w = jnp.exp2((s - jnp.concatenate([top] * (s.shape[1] // hd), axis=1)) * scale)
            summed = jnp.dot(w.astype(jnp.bfloat16), v_now, preferred_element_type=jnp.float32)
            if not first:
                fade = jnp.exp2((old - top) * scale)
                summed = acc[at] * jnp.concatenate([fade, fade], axis=1) + summed
            acc[at] = summed
            m_ref[at] = top
            return carry

        lax.fori_loop(0, heads // UNROLL, some_heads, 0)

    def causal():
        t_at = lax.rem(lax.broadcasted_iota(jnp.int32, (rows_q, span), 0), span)
        s_at = lax.broadcasted_iota(jnp.int32, (rows_q, span), 1)
        return jnp.where(s_at <= t_at, 0.0, LOW)

    attend(lambda col: nk_ref[:, pl.ds(col, hd)], lambda col: nv_ref[:, pl.ds(col, hd)], causal, True)

    own_block = lax.div(me, per_block)
    sent = 0
    for i in range(n // per_block):
        for d in range(i * per_block, (i + 1) * per_block):
            if d in far:
                for _ in range(2):
                    if sent + window < len(queue):
                        page_copy(*queue[sent]).wait_send()
                        page_copy(*queue[sent + window]).start()
                        sent += 1
        for d in range(i * per_block, (i + 1) * per_block):
            if d:
                page_copy(d, 0).wait_recv()
                page_copy(d, 1).wait_recv()
        base = pl.multiple_of(flipped(own_block, i) * block, block)

        attend(
            lambda col: recv[0, pl.ds(base, block), pl.ds(col, hd)],
            lambda col: recv[1, pl.ds(base, block), pl.ds(col, hd)],
            lambda: bias_ref[:, pl.ds(base, block)],
            False,
        )

    def finish(c, carry):
        value = acc[pl.ds(pl.multiple_of(c * span, span), span)]
        out_ref[:, pl.ds(pl.multiple_of(c * hd, hd), hd)] = (
            value[:, :hd] / value[:, hd:]
        ).astype(jnp.bfloat16)
        return carry

    lax.fori_loop(0, heads, finish, 0)

    for d in order:
        table_copy(d).wait_send()
        row_copy(d).wait()
    for d, half in queue[sent:] + [(d, half) for d in near for half in range(2)]:
        page_copy(d, half).wait_send()


def ranks(owner):
    at = jnp.arange(owner.shape[0], dtype=jnp.int32)
    same = owner[:, None] == owner[None, :]
    return jnp.sum(same & (at[None, :] < at[:, None]), axis=1, dtype=jnp.int32)


def shards(
    queries,
    new_keys,
    new_values,
    key_pool,
    value_pool,
    page_key_scale,
    value_scale,
    page_owner,
    page_slot,
    prefix_len,
    dec_owner,
    dec_slot,
    decode_keys,
    decode_values,
):
    n = lax.axis_size("pool")
    page_count = page_owner.shape[1]
    rows = page_count // n
    span = queries.shape[0]
    dec_rows = span // n
    dec_pad = -(-2 * dec_rows // 16) * 16
    columns = new_keys.shape[1]
    kv_heads = page_key_scale.shape[1]
    hd = columns // kv_heads
    group = queries.shape[1] // columns
    pool_pages, page_tok, _ = key_pool.shape
    keys = rows * page_tok

    owner, slot = page_owner[0], page_slot[0]
    place = owner * rows + ranks(owner)
    hit = place[None, :] == jnp.arange(page_count, dtype=jnp.int32)[:, None]
    slots = jnp.sum(jnp.where(hit, slot[None, :], 0), axis=1).reshape(n, rows)
    pages = jnp.sum(
        jnp.where(hit, jnp.arange(page_count, dtype=jnp.int32)[None, :], 0), axis=1
    )
    position = pages[:, None] * page_tok + jnp.arange(page_tok, dtype=jnp.int32)[None, :]
    bias = jnp.where(position.reshape(page_count * page_tok) < prefix_len[0], 0.0, LOW)
    bias = bias.astype(jnp.float32)[None, :]

    d_owner, d_slot = dec_owner[0], dec_slot[0]
    d_rank = ranks(d_owner)
    d_hit = (d_owner * dec_rows + d_rank)[None, :] == jnp.arange(span, dtype=jnp.int32)[:, None]
    d_slots = jnp.sum(jnp.where(d_hit, d_slot[None, :], 0), axis=1).reshape(n, dec_rows)
    placed = (d_owner * dec_pad + d_rank)[None, :]

    table = jnp.concatenate(
        [
            slots,
            jnp.zeros((n, TABLE_ROWS_AT - rows), jnp.int32),
            d_slots,
            jnp.zeros((n, 128 - TABLE_ROWS_AT - dec_rows), jnp.int32),
        ],
        axis=1,
    ).reshape(n, 1, 128)
    key_scale = jnp.repeat(page_key_scale.astype(jnp.float32), hd, axis=1)[:, None, :]
    val_scale = jnp.repeat(value_scale.astype(jnp.float32), hd, axis=1)[:, None, :]

    heads = kv_heads * group
    vmem = pl.BlockSpec(memory_space=pltpu.VMEM)
    attended, come, table_in = pl.pallas_call(
        functools.partial(
            kernel, n, rows, page_tok, dec_rows, dec_pad, kv_heads, group
        ),
        out_shape=(
            jax.ShapeDtypeStruct(queries.shape, jnp.bfloat16),
            jax.ShapeDtypeStruct((n, dec_pad, columns), jnp.bfloat16),
            jax.ShapeDtypeStruct((n, 1, 128), jnp.int32),
        ),
        in_specs=[vmem] * 10,
        out_specs=(vmem, vmem, vmem),
        scratch_shapes=[
            pltpu.SMEM((n, 1, 128), jnp.int32),
            pltpu.VMEM((n, 2, keys, columns), jnp.bfloat16),
            pltpu.VMEM((2, n * keys, columns), jnp.bfloat16),
            pltpu.VMEM((n, dec_pad, columns), jnp.bfloat16),
            pltpu.VMEM((heads * span, hd), jnp.bfloat16),
            pltpu.VMEM((heads * span, 2 * hd), jnp.float32),
            pltpu.VMEM((heads * span, hd), jnp.float32),
            pltpu.SemaphoreType.DMA((n,)),
            pltpu.SemaphoreType.DMA((n,)),
            pltpu.SemaphoreType.DMA((2, n)),
            pltpu.SemaphoreType.DMA((2, n)),
            pltpu.SemaphoreType.DMA((n,)),
            pltpu.SemaphoreType.DMA((n,)),
            pltpu.SemaphoreType.DMA,
        ],
        compiler_params=pltpu.CompilerParams(
            collective_id=0, has_side_effects=True, vmem_limit_bytes=52 * 1024 * 1024
        ),
        cost_estimate=pl.CostEstimate(
            flops=4 * span * heads * hd * (n * keys + span),
            bytes_accessed=16 * 1024 * 1024,
            transcendentals=span * heads * (n * keys + span),
        ),
    )(
        table,
        placed,
        queries,
        new_keys,
        new_values,
        key_pool,
        value_pool,
        key_scale,
        val_scale,
        bias,
    )

    come_slot = table_in[:, 0, TABLE_ROWS_AT : TABLE_ROWS_AT + dec_rows].reshape(span)
    put = jnp.arange(decode_keys.shape[0], dtype=jnp.int32)[:, None] == come_slot[None, :]
    touched = jnp.any(put, axis=1)[:, None]
    put = put.astype(jnp.bfloat16)
    come_keys = come[:, :dec_rows].reshape(span, columns)
    come_values = come[:, dec_rows : 2 * dec_rows].reshape(span, columns)
    keys_out = jnp.where(
        touched,
        jnp.dot(put, come_keys, preferred_element_type=jnp.float32).astype(jnp.bfloat16),
        decode_keys,
    )
    values_out = jnp.where(
        touched,
        jnp.dot(put, come_values, preferred_element_type=jnp.float32).astype(jnp.bfloat16),
        decode_values,
    )
    return attended, keys_out, values_out


def solution(mesh):
    two = P(("groups", "pool"), "tp")
    three = P(("groups", "pool"), None, "tp")
    table = P(("groups", "pool"), None)
    in_specs = (two, two, two, three, three, two, two, table, table)
    in_specs += (P(("groups", "pool")), table, table, two, two)
    return jax.shard_map(
        shards, mesh=mesh, in_specs=in_specs, out_specs=(two, two, two), check_vma=False
    )
```
